32 devices in a mesh: vocab: 16 (over z, y, x), batch: 2 (over core).
Axes of the slice: x: 2, y: 2, z: 4, core: 2. Of those that a mesh axis runs over, the one named last changes fastest.
Arguments:
- hidden: bfloat16 [256, 4096], P('batch', 'vocab'), may hold values from -6 to 6
- head_weight: bfloat16 [4096, 65536], P('batch', 'vocab'), may hold values from -0.09375 to 0.09375
- passages: bfloat16 [512, 65536], P('batch', 'vocab'), may hold values from -6 to 6
- pair_query: int32 [768], P('batch'), may hold values from 0 to 15
- pair_passage: int32 [768], P('batch'), may hold values from 0 to 255
- pair_count: int32 [2], P('batch'), may hold values from 128 to 384, as said below
- teacher: float32 [768], P('batch'), may hold values from -24 to 24
Outputs:
- pooled: bfloat16 [16, 65536], P('batch', 'vocab')
- grad_hidden: bfloat16 [256, 4096], P('batch', 'vocab')
- loss_value: float32 [], replicated
The draws below stay inside these ranges and needn't reach their ends.
Inputs may be any that keep to these rules, and one draw needn't show every extreme that they name: `pair_count`: slots of a group at or past its count are padding; some group has all 384 slots live.
All inputs are finite; a program needn't handle non-finite values.
Results may differ from the reference program's by a relative error of at most 0.012.
Values may be sent and summed in bfloat16 or wider, within the bound.
A program may use at most 128 MiB of HBM per device.

```python
import math
import jax
import jax.numpy as jnp
from jax import lax

D = 4096
VOCAB = 65536
QLEN = 16
PG = 256
SLOTS = 384
TOKENS = 256
QUERIES = 16
PASSAGES = 512
N_BATCH = 2


def draw_pair_count(key, part):
    first_key = jax.random.fold_in(key, 11)
    second_key = jax.random.fold_in(key, 23)
    counts = jax.random.randint(first_key, (N_BATCH,), SLOTS // 3, SLOTS + 1)
    chosen = jax.random.randint(second_key, (), 0, N_BATCH)
    return jnp.where(jnp.arange(N_BATCH) == chosen, SLOTS, counts).astype(jnp.int32)


def touch_ends(array, stream_key, least, high):
    longest = array.shape.index(max(array.shape))
    spots = []
    for shift in (0, 1):
        where = [jax.random.randint(jax.random.fold_in(stream_key, axis), (), 0, length) for axis, length in enumerate(array.shape)]
        where[longest] = (where[longest] + shift) % array.shape[longest]
        spots.append(tuple(where))
    return array.at[spots[0]].set(least).at[spots[1]].set(high)


def steps_of(stream_key, shape, cuts, smallest, high):
    factor_of, own = 1.0, jax.random.fold_in(stream_key, 6)
    for dim, blocks in cuts:
        heights = jnp.exp(jax.random.uniform(jax.random.fold_in(own, dim), (blocks,), jnp.float32, smallest / len(cuts), high / len(cuts)))
        factor_of = factor_of * jnp.repeat(heights, shape[dim] // blocks).reshape([-1 if axis == dim else 1 for axis in range(len(shape))])
    return factor_of


def bell_draw(own_key, extent, scale, limit, shards=(), kind=jnp.bfloat16):
    drawn = scale * jax.random.normal(own_key, extent, jnp.float32)
    if shards:
        drawn = drawn * steps_of(own_key, extent, shards, -0.22, 0.18)
    return jnp.clip(drawn, -limit, limit).astype(kind)


def setup_inputs(seed: int = 0) -> dict:
    key_list = jax.random.split(jax.random.key(seed), 8)
    return {
        "hidden": bell_draw(key_list[0], (TOKENS, D), 1.0, 6.0, ((0, 2), (1, 16))),
        "head_weight": bell_draw(key_list[1], (D, VOCAB), D ** -0.5, 0.09375, ((0, 2), (1, 16))),
        "passages": bell_draw(key_list[2], (PASSAGES, VOCAB), 1.0, 6.0, ((0, 2), (1, 16))),
        "pair_query": touch_ends(jax.random.randint(key_list[3], (N_BATCH * SLOTS,), 0, QUERIES), jax.random.fold_in(key_list[3], 1), 0, QUERIES - 1).astype(jnp.int32),
        "pair_passage": touch_ends(jax.random.randint(key_list[4], (N_BATCH * SLOTS,), 0, PG), jax.random.fold_in(key_list[4], 1), 0, PG - 1).astype(jnp.int32),
        "pair_count": draw_pair_count(jax.random.fold_in(key_list[7], 71), 0),
        "teacher": bell_draw(key_list[6], (N_BATCH * SLOTS,), 4.0, 24.0, ((0, 2),), jnp.float32),
    }


def saturate(logits):
    positive = jnp.maximum(logits, 0.0)
    return (jnp.log1p(positive), jnp.where(logits > 0, 1.0 / (1.0 + positive), 0.0))

def reference(hidden, head_weight, passages, pair_query, pair_passage, pair_count, teacher):
    block_size = math.gcd(VOCAB, 4096)
    block_count = VOCAB // block_size
    head_blocks = head_weight.reshape(D, block_count, block_size).transpose(1, 0, 2)

    def forward_block(weights):
        logits = jnp.dot(hidden, weights, preferred_element_type=jnp.float32)
        saturated, unused = saturate(logits)
        return saturated.reshape(QUERIES, QLEN, block_size).sum(1).astype(jnp.bfloat16)
    pooled_blocks = lax.map(forward_block, head_blocks)
    pooled = pooled_blocks.transpose(1, 0, 2).reshape(QUERIES, VOCAB)
    score_table = jnp.dot(pooled, passages.T, preferred_element_type=jnp.float32)
    inv_root = 1.0 / math.sqrt(VOCAB)
    slot_ids = jnp.arange(N_BATCH * SLOTS, dtype=jnp.int32)
    group_index = slot_ids // SLOTS
    slot_index = slot_ids % SLOTS
    global_passage = (group_index * PG + pair_passage).astype(jnp.int32)
    scores = score_table[pair_query, global_passage] * inv_root
    is_live = slot_index < pair_count[group_index]
    residual = jnp.where(is_live, scores - teacher, 0.0)
    loss_value = jnp.sum(residual * residual) / (SLOTS * N_BATCH)
    pair_grad = 2.0 * residual * inv_root
    pair_table = jnp.zeros((QUERIES, PASSAGES), jnp.float32).at[pair_query, global_passage].add(pair_grad)
    query_grad = jnp.dot(pair_table, passages.astype(jnp.float32), precision=lax.Precision.HIGHEST)
    query_blocks = query_grad.reshape(QUERIES, block_count, block_size).transpose(1, 0, 2)

    def backward_block(carry, items):
        weights, query_block = items
        logits = jnp.dot(hidden, weights, preferred_element_type=jnp.float32)
        unused, slope_term = saturate(logits)
        logit_grad = (jnp.repeat(query_block, QLEN, axis=0) * slope_term).astype(jnp.bfloat16)
        return (carry + jnp.dot(logit_grad, weights.T, preferred_element_type=jnp.float32), None)
    grad_total, unused = lax.scan(backward_block, jnp.zeros((TOKENS, D), jnp.float32), (head_blocks, query_blocks))
    return (pooled, grad_total.astype(jnp.bfloat16), loss_value)
```

```python
import functools
import math

import jax
import jax.numpy as jnp
from jax import lax
from jax.experimental import pallas as pl
from jax.experimental.pallas import tpu as pltpu
from jax.sharding import PartitionSpec as P

VOCAB = 65536
QLEN = 16


def plain(hidden, head_weight, passages, pair_query, pair_passage, pair_count, teacher):
    features = lax.all_gather(hidden, "vocab", axis=1, tiled=True)
    full_head = lax.all_gather(head_weight, "batch", axis=0, tiled=True)
    logits = jnp.dot(features, full_head, preferred_element_type=jnp.float32)
    positive = jnp.maximum(logits, 0.0)
    saturated = jnp.log1p(positive)
    tok_count, col_count = logits.shape
    query_count = tok_count // QLEN
    pooled = saturated.reshape(query_count, QLEN, col_count).sum(1).astype(jnp.bfloat16)
    every_query = lax.all_gather(pooled, "batch", axis=0, tiled=True)
    score_table = jnp.dot(every_query, passages.T, preferred_element_type=jnp.float32)
    partial_value = score_table[pair_query, pair_passage]
    inv_root = 1.0 / math.sqrt(VOCAB)
    slot_count = pair_query.shape[0]
    is_live = jnp.arange(slot_count, dtype=jnp.int32) < pair_count[0]
    scores = lax.psum(partial_value, "vocab") * inv_root
    residual = jnp.where(is_live, scores - teacher, 0.0)
    error_total = lax.psum(jnp.sum(residual * residual), "batch")
    pair_grad = 2.0 * residual * inv_root
    loss_value = error_total / (slot_count * lax.axis_size("batch"))
    query_onehot = (
        pair_query[:, None] == jnp.arange(every_query.shape[0], dtype=jnp.int32)[None, :]
    ).astype(jnp.float32)
    passage_onehot = (
        pair_passage[:, None] == jnp.arange(passages.shape[0], dtype=jnp.int32)[None, :]
    ).astype(jnp.float32)
    pair_table = jnp.dot(
        query_onehot.T, passage_onehot * pair_grad[:, None], precision=lax.Precision.HIGHEST
    )
    table_high = pair_table.astype(jnp.bfloat16)
    table_low = (pair_table - table_high.astype(jnp.float32)).astype(jnp.bfloat16)
    query_terms = jnp.dot(table_high, passages, preferred_element_type=jnp.float32) + jnp.dot(
        table_low, passages, preferred_element_type=jnp.float32
    )
    query_grad = lax.psum_scatter(query_terms, "batch", scatter_dimension=0, tiled=True)
    slope_term = jnp.where(logits > 0, 1.0 / (1.0 + positive), 0.0)
    spread_grad = jnp.broadcast_to(query_grad[:, None, :], (query_count, QLEN, col_count)).reshape(
        tok_count, col_count
    )
    logit_grad = (spread_grad * slope_term).astype(jnp.bfloat16)
    hidden_terms = lax.dot_general(
        logit_grad, full_head, (((1,), (1,)), ((), ())), preferred_element_type=jnp.float32
    )
    grad_hidden = lax.psum_scatter(hidden_terms, "vocab", scatter_dimension=1, tiled=True).astype(
        jnp.bfloat16
    )
    return (pooled, grad_hidden, loss_value)


MESH = pl.DeviceIdType.MESH
HIGHEST = lax.Precision.HIGHEST
NT_DIMS = (((1,), (1,)), ((), ()))


def device(v, b):
    return (v, b)


def landed(ref, sem):
    pltpu.make_async_copy(ref, ref, sem).wait()


def remote(src, dst, send, recv, to):
    return pltpu.make_async_remote_copy(
        src_ref=src, dst_ref=dst, send_sem=send, recv_sem=recv, device_id=to, device_id_type=MESH
    )


def kernel(
    n_vocab, n_planes, n_in, tiles,
    hid, head, pas, pair_q, pair_p, count, teacher,
    pooled_out, grad_out, loss_out,
    head_v, pas_v, feat, part, part_in, every_q, terms, terms_in, lgrad,
    hidden_out, from_plane, plane_sum, from_column, plane_scores, column_scores, errors,
    head_s, pas_s, col_send, feat_recv, plane_send, part_send, part_recv, pool_send, pool_recv,
    terms_send, terms_recv, lgrad_send, lgrad_recv, ps_send, ps_recv, cs_send, cs_recv,
    err_send, err_recv, x_send, x_recv, y_send, y_recv,
):
    tok, width = hid.shape
    slots = pair_q.shape[1]
    pg = pas.shape[0]
    rows, cols = head.shape
    ct = cols // tiles
    blocks = rows // width
    zb = blocks // n_in
    queries = tok // QLEN
    v, b = lax.axis_index("vocab"), lax.axis_index("batch")
    z, r = v // n_in, v % n_in
    other = 1 - b
    peer = (v, other)
    inv_root = 1.0 / math.sqrt(cols * n_vocab)

    def plane_peer(s):
        return (z * n_in + (r + s) % n_in, b)

    def column_index(dz):
        return ((z + dz) % n_planes) * n_in + r

    def head_copy(t):
        return pltpu.make_async_copy(
            head.at[:, pl.ds(pl.multiple_of(t * ct, ct), ct)], head_v.at[t], head_s.at[t]
        )

    def pas_copy(t):
        return pltpu.make_async_copy(
            pas.at[:, pl.ds(pl.multiple_of(t * ct, ct), ct)], pas_v.at[t], pas_s.at[t]
        )

    barrier = pltpu.get_barrier_semaphore()
    for s in range(1, n_in):
        pl.semaphore_signal(barrier, inc=1, device_id=plane_peer(s), device_id_type=MESH)
    for dz in range(n_planes):
        if dz:
            pl.semaphore_signal(barrier, inc=1, device_id=(column_index(dz), b), device_id_type=MESH)
        pl.semaphore_signal(barrier, inc=1, device_id=(column_index(dz), other), device_id_type=MESH)

    @pl.loop(0, tiles)
    def _(t):
        head_copy(t).start()

    @pl.loop(0, tiles)
    def _(t):
        pas_copy(t).start()

    pl.semaphore_wait(barrier, n_in - 1 + 2 * n_planes - 1)

    def feat_at(j, half):
        return feat.at[
            pl.ds(pl.multiple_of(half * tok, tok), tok), pl.ds(pl.multiple_of(j * width, width), width)
        ]

    goal = v // blocks
    mine = v % blocks

    def column_copy(dz):
        return remote(
            hid, feat_at(mine, b), col_send.at[dz], feat_recv.at[mine * 2 + b], (column_index(dz), goal)
        )

    def own_feat():
        return pltpu.make_async_copy(hid, feat_at(mine, b), feat_recv.at[mine * 2 + b])

    def own_to_peer():
        return remote(hid, feat_at(mine, b), col_send.at[0], feat_recv.at[mine * 2 + b], peer)

    for dz in [2, 1, 3] if n_planes == 4 else range(1, n_planes):
        column_copy(dz).start()

    @pl.when(goal == b)
    def _():
        own_feat().start()

    @pl.when(goal != b)
    def _():
        own_to_peer().start()

    def plane_copy(zz, half, s):
        j = zz * n_in + r
        return remote(
            feat_at(j, half),
            feat_at(j, half),
            plane_send.at[(zz * 2 + half) * (n_in - 1) + s - 1],
            feat_recv.at[j * 2 + half],
            plane_peer(s),
        )

    for zz in range(zb):
        for half in range(2):
            j = zz * n_in + r
            landed(feat_at(j, half), feat_recv.at[j * 2 + half])
            for s in range(1, n_in):
                plane_copy(zz, half, s).start()
    for zz in range(zb):
        for half in range(2):
            for s in range(1, n_in):
                j = zz * n_in + (r + s) % n_in
                landed(feat_at(j, half), feat_recv.at[j * 2 + half])

    own_rows = pl.ds(pl.multiple_of(b * tok, tok), tok)
    peer_rows = pl.ds(pl.multiple_of(other * tok, tok), tok)

    def part_copy(t):
        return remote(part.at[t, peer_rows], part_in.at[t], part_send.at[t], part_recv.at[t], peer)

    @pl.loop(0, tiles)
    def _(t):
        head_copy(t).wait()
        part[t] = jnp.dot(feat[...], head_v[t], preferred_element_type=jnp.float32)
        part_copy(t).start()

    def pool_copy(t):
        return remote(every_q.at[b, t], every_q.at[b, t], pool_send.at[t], pool_recv.at[t], peer)

    @pl.loop(0, tiles)
    def _(t):
        landed(part_in.at[t], part_recv.at[t])
        logits = part[t, own_rows, :] + part_in[t]
        part[t, own_rows, :] = logits
        saturated = jnp.log1p(jnp.maximum(logits, 0.0))
        pooled = saturated.reshape(queries, QLEN, ct).sum(1).astype(jnp.bfloat16)
        pooled_out[:, pl.ds(pl.multiple_of(t * ct, ct), ct)] = pooled
        every_q[b, t] = pooled.astype(jnp.float32)
        pool_copy(t).start()

    def table_step(t, table):
        pas_copy(t).wait()
        landed(every_q.at[other, t], pool_recv.at[t])
        both = jnp.concatenate([every_q[0, t], every_q[1, t]], axis=0).astype(jnp.bfloat16)
        return table + lax.dot_general(both, pas_v[t], NT_DIMS, preferred_element_type=jnp.float32)

    table = lax.fori_loop(0, tiles, table_step, jnp.zeros((2 * queries, pg), jnp.float32))
    hot_p = (pair_p[...] == lax.broadcasted_iota(jnp.int32, (pg, slots), 0)).astype(jnp.float32)
    hot_q = (pair_q[...] == lax.broadcasted_iota(jnp.int32, (2 * queries, slots), 0)).astype(
        jnp.float32
    )
    picked = jnp.dot(table, hot_p, precision=HIGHEST, preferred_element_type=jnp.float32)
    plane_scores[r] = jnp.sum(picked * hot_q, axis=0, keepdims=True)

    def plane_score_copy(s):
        return remote(
            plane_scores.at[r], plane_scores.at[r], ps_send.at[s - 1], ps_recv.at[r], plane_peer(s)
        )

    def column_score_copy(dz):
        return remote(
            column_scores.at[z], column_scores.at[z], cs_send.at[dz - 1], cs_recv.at[z],
            (column_index(dz), b),
        )

    for s in range(1, n_in):
        plane_score_copy(s).start()
    for s in range(1, n_in):
        landed(plane_scores.at[(r + s) % n_in], ps_recv.at[(r + s) % n_in])
    column_scores[z] = jnp.sum(plane_scores[...], axis=0)
    for dz in range(1, n_planes):
        column_score_copy(dz).start()
    for dz in range(1, n_planes):
        landed(column_scores.at[(z + dz) % n_planes], cs_recv.at[(z + dz) % n_planes])
    scores = jnp.sum(column_scores[...], axis=0) * inv_root

    is_live = lax.broadcasted_iota(jnp.int32, (1, slots), 1) < count[...]
    residual = jnp.where(is_live, scores - teacher[...], 0.0)
    error = jnp.sum(residual * residual, axis=1, keepdims=True)
    errors[b] = jnp.broadcast_to(error, errors.shape[1:])
    err_copy = remote(errors.at[b], errors.at[b], err_send.at[0], err_recv.at[0], peer)
    err_copy.start()
    pair_grad = 2.0 * residual * inv_root
    pair_table = lax.dot_general(
        hot_q * pair_grad, hot_p, NT_DIMS, precision=HIGHEST, preferred_element_type=jnp.float32
    )
    high = pair_table.astype(jnp.bfloat16)
    low = (pair_table - high.astype(jnp.float32)).astype(jnp.bfloat16)
    split = jnp.concatenate([high, low], axis=0)

    def terms_copy(t):
        return remote(terms.at[other, t], terms_in.at[t], terms_send.at[t], terms_recv.at[t], peer)

    @pl.loop(0, tiles)
    def _(t):
        both = jnp.dot(split, pas_v[t], preferred_element_type=jnp.float32)
        whole = both[: 2 * queries] + both[2 * queries :]
        terms[0, t] = whole[:queries]
        terms[1, t] = whole[queries:]
        terms_copy(t).start()

    def lgrad_copy(t):
        return remote(
            lgrad.at[t, own_rows], lgrad.at[t, own_rows], lgrad_send.at[t], lgrad_recv.at[t], peer
        )

    @pl.loop(0, tiles)
    def _(t):
        landed(terms_in.at[t], terms_recv.at[t])
        query_grad = terms[b, t] + terms_in[t]
        logits = part[t, own_rows, :]
        slope = jnp.where(logits > 0, 1.0 / (1.0 + jnp.maximum(logits, 0.0)), 0.0)
        spread = jnp.broadcast_to(query_grad[:, None, :], (queries, QLEN, ct)).reshape(tok, ct)
        lgrad[t, own_rows, :] = (spread * slope).astype(jnp.bfloat16)
        lgrad_copy(t).start()

    @pl.loop(0, tiles)
    def _(t):
        landed(lgrad.at[t, peer_rows], lgrad_recv.at[t])

    def hidden_block(j):
        block = pl.ds(pl.multiple_of(j * width, width), width)
        total = jnp.zeros((2 * tok, width), jnp.float32)
        for t in range(tiles):
            total += lax.dot_general(
                lgrad[t], head_v[t, block, :], NT_DIMS, preferred_element_type=jnp.float32
            )
        return total.reshape(2, tok, width)

    def x_copy(zz, s):
        return remote(
            hidden_out.at[zz, s - 1],
            from_plane.at[zz, s - 1],
            x_send.at[zz * (n_in - 1) + s - 1],
            x_recv.at[zz * (n_in - 1) + s - 1],
            plane_peer(s),
        )

    @pl.loop(0, zb * (n_in - 1))
    def _(i):
        s, zz = n_in - 1 - i // zb, i % zb
        hidden_out[zz, s - 1] = hidden_block(zz * n_in + (r + s) % n_in).astype(jnp.bfloat16)
        x_copy(zz, s).start()

    def y_copy(zz, half):
        return remote(
            plane_sum.at[zz, half],
            from_column.at[z],
            y_send.at[zz * 2 + half],
            y_recv.at[z],
            ((b * zb + zz) * n_in + r, half),
        )

    def y_here(zz, half):
        return pltpu.make_async_copy(plane_sum.at[zz, half], from_column.at[z], y_recv.at[z])

    def y_is_here(zz, half):
        return jnp.logical_and(b * zb + zz == z, b == half)

    @pl.loop(0, zb)
    def _(zz):
        total = hidden_block(zz * n_in + r)
        for s in range(n_in - 1, 0, -1):
            landed(from_plane.at[zz, s - 1], x_recv.at[zz * (n_in - 1) + s - 1])
            total += from_plane[zz, s - 1].astype(jnp.float32)
        plane_sum[zz] = total.astype(jnp.bfloat16)
        for half in range(2):

            @pl.when(y_is_here(zz, half))
            def _():
                y_here(zz, half).start()

            @pl.when(jnp.logical_not(y_is_here(zz, half)))
            def _():
                y_copy(zz, half).start()

    total = jnp.zeros((tok, width), jnp.float32)
    for k in range(n_planes):
        landed(from_column.at[k], y_recv.at[k])
        total += from_column[k].astype(jnp.float32)
    grad_out[...] = total.astype(jnp.bfloat16)

    landed(errors.at[other], err_recv.at[0])
    loss_out[...] = (errors[0] + errors[1]) / (slots * 2)

    for dz in range(1, n_planes):
        column_copy(dz).wait_send()
        column_score_copy(dz).wait_send()

    @pl.when(goal != b)
    def _():
        own_to_peer().wait_send()

    for s in range(1, n_in):
        plane_score_copy(s).wait_send()
        for zz in range(zb):
            x_copy(zz, s).wait_send()
            for half in range(2):
                plane_copy(zz, half, s).wait_send()
    err_copy.wait_send()
    for zz in range(zb):
        for half in range(2):

            @pl.when(jnp.logical_not(y_is_here(zz, half)))
            def _():
                y_copy(zz, half).wait_send()

    @pl.loop(0, tiles)
    def _(t):
        part_copy(t).wait_send()
        pool_copy(t).wait_send()
        terms_copy(t).wait_send()
        lgrad_copy(t).wait_send()


def inner_axis(n_vocab):
    size = 1
    while size * size < n_vocab:
        size *= 2
    return size


def fused(n_vocab, hidden, head_weight, passages, pair_query, pair_passage, pair_count, teacher):
    tok, width = hidden.shape
    rows, cols = head_weight.shape
    pg = passages.shape[0]
    slots = pair_query.shape[0]
    n_in = inner_axis(n_vocab)
    n_planes = n_vocab // n_in
    blocks = rows // width
    zb = blocks // n_in
    ct = math.gcd(cols, 512)
    tiles = cols // ct
    queries = tok // QLEN
    vmem = pl.BlockSpec(memory_space=pltpu.VMEM)
    hbm = pl.BlockSpec(memory_space=pl.ANY)
    bf16, f32 = jnp.bfloat16, jnp.float32
    dma = pltpu.SemaphoreType.DMA
    pooled, grad, loss = pl.pallas_call(
        functools.partial(kernel, n_vocab, n_planes, n_in, tiles),
        out_shape=(
            jax.ShapeDtypeStruct((queries, cols), bf16),
            jax.ShapeDtypeStruct((tok, width), bf16),
            jax.ShapeDtypeStruct((1, 128), f32),
        ),
        in_specs=[vmem, hbm, hbm, vmem, vmem, vmem, vmem],
        out_specs=(vmem, vmem, vmem),
        scratch_shapes=[
            pltpu.VMEM((tiles, rows, ct), bf16),
            pltpu.VMEM((tiles, pg, ct), bf16),
            pltpu.VMEM((2 * tok, rows), bf16),
            pltpu.VMEM((tiles, 2 * tok, ct), f32),
            pltpu.VMEM((tiles, tok, ct), f32),
            pltpu.VMEM((2, tiles, queries, ct), f32),
            pltpu.VMEM((2, tiles, queries, ct), f32),
            pltpu.VMEM((tiles, queries, ct), f32),
            pltpu.VMEM((tiles, 2 * tok, ct), bf16),
            pltpu.VMEM((zb, n_in - 1, 2, tok, width), bf16),
            pltpu.VMEM((zb, n_in - 1, 2, tok, width), bf16),
            pltpu.VMEM((zb, 2, tok, width), bf16),
            pltpu.VMEM((n_planes, tok, width), bf16),
            pltpu.VMEM((n_in, 1, slots), f32),
            pltpu.VMEM((n_planes, 1, slots), f32),
            pltpu.VMEM((2, 1, 128), f32),
            dma((tiles,)), dma((tiles,)),
            dma((n_planes,)), dma((2 * blocks,)), dma((2 * zb * (n_in - 1),)),
            dma((tiles,)), dma((tiles,)), dma((tiles,)), dma((tiles,)),
            dma((tiles,)), dma((tiles,)), dma((tiles,)), dma((tiles,)),
            dma((n_in - 1,)), dma((n_in,)), dma((n_planes - 1,)), dma((n_planes,)),
            dma((1,)), dma((1,)),
            dma((zb * (n_in - 1),)), dma((zb * (n_in - 1),)),
            dma((2 * zb,)), dma((n_planes,)),
        ],
        compiler_params=pltpu.CompilerParams(
            collective_id=0, has_side_effects=True, vmem_limit_bytes=52 * 1024 * 1024
        ),
        cost_estimate=pl.CostEstimate(
            flops=8 * tok * rows * cols,
            bytes_accessed=2 * rows * cols + 2 * pg * cols,
            transcendentals=tok * cols,
        ),
    )(
        hidden, head_weight, passages,
        pair_query.reshape(1, slots), pair_passage.reshape(1, slots),
        pair_count.reshape(1, 1), teacher.reshape(1, slots),
    )
    return (pooled, grad, loss[0, 0])


def local(n_vocab, n_batch, hidden, head_weight, *rest):
    width, rows, cols = hidden.shape[1], head_weight.shape[0], head_weight.shape[1]
    n_in = inner_axis(n_vocab)
    if (
        n_batch == 2
        and n_vocab % n_in == 0
        and (rows // width) % n_in == 0
        and width % 128 == 0
        and cols % 512 == 0
        and rows * cols <= 2**23
    ):
        return fused(n_vocab, hidden, head_weight, *rest)
    return plain(hidden, head_weight, *rest)


def solution(mesh):
    in_specs = (
        P("batch", "vocab"),
        P("batch", "vocab"),
        P("batch", "vocab"),
        P("batch"),
        P("batch"),
        P("batch"),
        P("batch"),
    )
    out_specs = (P("batch", "vocab"), P("batch", "vocab"), P())
    body = functools.partial(local, mesh.shape["vocab"], mesh.shape["batch"])
    return jax.shard_map(
        body, mesh=mesh, in_specs=in_specs, out_specs=out_specs, check_vma=False)
```

```python
import functools
import math

import jax
import jax.numpy as jnp
from jax import lax
from jax.experimental import pallas as pl
from jax.experimental.pallas import tpu as pltpu
from jax.sharding import PartitionSpec as P

VOCAB = 65536
QLEN = 16


def plain(hidden, head_weight, passages, pair_query, pair_passage, pair_count, teacher):
    features = lax.all_gather(hidden, "vocab", axis=1, tiled=True)
    full_head = lax.all_gather(head_weight, "batch", axis=0, tiled=True)
    logits = jnp.dot(features, full_head, preferred_element_type=jnp.float32)
    positive = jnp.maximum(logits, 0.0)
    saturated = jnp.log1p(positive)
    tok_count, col_count = logits.shape
    query_count = tok_count // QLEN
    pooled = saturated.reshape(query_count, QLEN, col_count).sum(1).astype(jnp.bfloat16)
    every_query = lax.all_gather(pooled, "batch", axis=0, tiled=True)
    score_table = jnp.dot(every_query, passages.T, preferred_element_type=jnp.float32)
    partial_value = score_table[pair_query, pair_passage]
    inv_root = 1.0 / math.sqrt(VOCAB)
    slot_count = pair_query.shape[0]
    is_live = jnp.arange(slot_count, dtype=jnp.int32) < pair_count[0]
    scores = lax.psum(partial_value, "vocab") * inv_root
    residual = jnp.where(is_live, scores - teacher, 0.0)
    error_total = lax.psum(jnp.sum(residual * residual), "batch")
    pair_grad = 2.0 * residual * inv_root
    loss_value = error_total / (slot_count * lax.axis_size("batch"))
    query_onehot = (
        pair_query[:, None] == jnp.arange(every_query.shape[0], dtype=jnp.int32)[None, :]
    ).astype(jnp.float32)
    passage_onehot = (
        pair_passage[:, None] == jnp.arange(passages.shape[0], dtype=jnp.int32)[None, :]
    ).astype(jnp.float32)
    pair_table = jnp.dot(
        query_onehot.T, passage_onehot * pair_grad[:, None], precision=lax.Precision.HIGHEST
    )
    table_high = pair_table.astype(jnp.bfloat16)
    table_low = (pair_table - table_high.astype(jnp.float32)).astype(jnp.bfloat16)
    query_terms = jnp.dot(table_high, passages, preferred_element_type=jnp.float32) + jnp.dot(
        table_low, passages, preferred_element_type=jnp.float32
    )
    query_grad = lax.psum_scatter(query_terms, "batch", scatter_dimension=0, tiled=True)
    slope_term = jnp.where(logits > 0, 1.0 / (1.0 + positive), 0.0)
    spread_grad = jnp.broadcast_to(query_grad[:, None, :], (query_count, QLEN, col_count)).reshape(
        tok_count, col_count
    )
    logit_grad = (spread_grad * slope_term).astype(jnp.bfloat16)
    hidden_terms = lax.dot_general(
        logit_grad, full_head, (((1,), (1,)), ((), ())), preferred_element_type=jnp.float32
    )
    grad_hidden = lax.psum_scatter(hidden_terms, "vocab", scatter_dimension=1, tiled=True).astype(
        jnp.bfloat16
    )
    return (pooled, grad_hidden, loss_value)


MESH = pl.DeviceIdType.MESH
HIGHEST = lax.Precision.HIGHEST
NT_DIMS = (((1,), (1,)), ((), ()))


def device(v, b):
    return (v, b)


def landed(ref, sem):
    pltpu.make_async_copy(ref, ref, sem).wait()


def remote(src, dst, send, recv, to):
    return pltpu.make_async_remote_copy(
        src_ref=src, dst_ref=dst, send_sem=send, recv_sem=recv, device_id=to, device_id_type=MESH
    )


def kernel(
    n_vocab, n_planes, n_in, tiles,
    hid, head, pas, pair_q, pair_p, count, teacher,
    pooled_out, grad_out, loss_out,
    head_v, pas_v, feat, part, part_in, every_q, terms, terms_in, lgrad,
    hidden_out, from_plane, own_sum, plane_sum, from_column, plane_scores, column_scores, errors,
    head_s, pas_s, col_send, feat_recv, plane_send, part_send, part_recv, pool_send, pool_recv,
    terms_send, terms_recv, lgrad_send, lgrad_recv, ps_send, ps_recv, cs_send, cs_recv,
    err_send, err_recv, x_send, x_recv, y_send, y_recv,
):
    tok, width = hid.shape
    slots = pair_q.shape[0]
    pg = pas.shape[0]
    rows, cols = head.shape
    ct = cols // tiles
    blocks = rows // width
    zb = blocks // n_in
    queries = tok // QLEN
    v, b = lax.axis_index("vocab"), lax.axis_index("batch")
    z, r = v // n_in, v % n_in
    other = 1 - b
    peer = (v, other)
    inv_root = 1.0 / math.sqrt(cols * n_vocab)

    def plane_peer(s):
        return (z * n_in + (r + s) % n_in, b)

    def column_index(dz):
        return ((z + dz) % n_planes) * n_in + r

    def head_copy(t):
        return pltpu.make_async_copy(
            head.at[:, pl.ds(pl.multiple_of(t * ct, ct), ct)], head_v.at[t], head_s.at[t]
        )

    def pas_copy(t):
        return pltpu.make_async_copy(
            pas.at[:, pl.ds(pl.multiple_of(t * ct, ct), ct)], pas_v.at[t], pas_s.at[t]
        )

    barrier = pltpu.get_barrier_semaphore()
    for s in range(1, n_in):
        pl.semaphore_signal(barrier, inc=1, device_id=plane_peer(s), device_id_type=MESH)
    for dz in range(n_planes):
        if dz:
            pl.semaphore_signal(barrier, inc=1, device_id=(column_index(dz), b), device_id_type=MESH)
        pl.semaphore_signal(barrier, inc=1, device_id=(column_index(dz), other), device_id_type=MESH)

    @pl.loop(0, tiles)
    def _(t):
        head_copy(t).start()

    @pl.loop(0, tiles)
    def _(t):
        pas_copy(t).start()

    pl.semaphore_wait(barrier, n_in - 1 + 2 * n_planes - 1)

    def feat_at(j, half):
        return feat.at[
            j // n_in,
            pl.ds(pl.multiple_of(half * tok, tok), tok),
            pl.ds(pl.multiple_of(j % n_in * width, width), width),
        ]

    goal = v // blocks
    mine = v % blocks

    def column_copy(dz):
        return remote(
            hid, feat_at(mine, b), col_send.at[dz], feat_recv.at[mine * 2 + b], (column_index(dz), goal)
        )

    def own_feat():
        return pltpu.make_async_copy(hid, feat_at(mine, b), feat_recv.at[mine * 2 + b])

    def own_to_peer():
        return remote(hid, feat_at(mine, b), col_send.at[0], feat_recv.at[mine * 2 + b], peer)

    for dz in [2, 1, 3] if n_planes == 4 else range(1, n_planes):
        column_copy(dz).start()

    @pl.when(goal == b)
    def _():
        own_feat().start()

    @pl.when(goal != b)
    def _():
        own_to_peer().start()

    def plane_copy(zz, half, s):
        j = zz * n_in + r
        return remote(
            feat_at(j, half),
            feat_at(j, half),
            plane_send.at[(zz * 2 + half) * (n_in - 1) + s - 1],
            feat_recv.at[j * 2 + half],
            plane_peer(s),
        )

    first = jnp.clip(z - zb * b, 0, zb - 1)
    for k in range(zb):
        for half in range(2):
            zz = (first + k) % zb
            j = zz * n_in + r
            landed(feat_at(j, half), feat_recv.at[j * 2 + half])
            for s in range(1, n_in):
                plane_copy(zz, half, s).start()

    def plane_landed(zz):
        for half in range(2):
            for s in range(1, n_in):
                j = zz * n_in + (r + s) % n_in
                landed(feat_at(j, half), feat_recv.at[j * 2 + half])

    def rows_product(zz, t):
        deep = rows // zb
        return jnp.dot(
            feat[zz],
            head_v[t, pl.ds(pl.multiple_of(zz * deep, deep), deep), :],
            preferred_element_type=jnp.float32,
        )

    own_rows = pl.ds(pl.multiple_of(b * tok, tok), tok)
    peer_rows = pl.ds(pl.multiple_of(other * tok, tok), tok)

    def part_copy(t):
        return remote(part.at[t, peer_rows], part_in.at[t], part_send.at[t], part_recv.at[t], peer)

    for k in range(zb - 1):
        zz = (first + k) % zb
        plane_landed(zz)

        @pl.loop(0, tiles)
        def _(t):
            if k == 0:
                head_copy(t).wait()
                part[t] = rows_product(zz, t)
            else:
                part[t] += rows_product(zz, t)

    last = (first + zb - 1) % zb
    plane_landed(last)

    def produce(t):
        if zb == 1:
            head_copy(t).wait()
            part[t] = rows_product(last, t)
        else:
            part[t] += rows_product(last, t)
        part_copy(t).start()

    def pool_copy(t):
        return remote(every_q.at[b, t], every_q.at[b, t], pool_send.at[t], pool_recv.at[t], peer)

    def consume(t):
        landed(part_in.at[t], part_recv.at[t])
        logits = part[t, own_rows, :] + part_in[t]
        positive = jnp.maximum(logits, 0.0)
        part[t, own_rows, :] = jnp.where(logits > 0, 1.0 / (1.0 + positive), 0.0)
        pooled = jnp.log1p(positive).reshape(queries, QLEN, ct).sum(1).astype(jnp.bfloat16)
        pooled_out[:, pl.ds(pl.multiple_of(t * ct, ct), ct)] = pooled
        every_q[b, t] = pooled.astype(jnp.float32)
        pool_copy(t).start()

    def table_step(t, table):
        pas_copy(t).wait()
        landed(every_q.at[other, t], pool_recv.at[t])
        both = jnp.concatenate([every_q[0, t], every_q[1, t]], axis=0).astype(jnp.bfloat16)
        return table + lax.dot_general(both, pas_v[t], NT_DIMS, preferred_element_type=jnp.float32)

    @pl.loop(0, 2)
    def _(t):
        produce(t)

    produce(2)
    consume(0)

    def forward_step(t, table):
        produce(t)
        consume(t - 2)
        return table_step(t - 3, table)

    def tail_step(t, table):
        consume(t)
        return table_step(t - 1, table)

    table = jnp.zeros((2 * queries, pg), jnp.float32)
    table = lax.fori_loop(3, tiles, forward_step, table)
    table = lax.fori_loop(tiles - 2, tiles, tail_step, table)
    table = table_step(tiles - 1, table)
    hot_p = (pair_p[...].reshape(1, slots) == lax.broadcasted_iota(jnp.int32, (pg, slots), 0)).astype(jnp.float32)
    hot_q = (pair_q[...].reshape(1, slots) == lax.broadcasted_iota(jnp.int32, (2 * queries, slots), 0)).astype(
        jnp.float32
    )
    picked = jnp.dot(table, hot_p, precision=HIGHEST, preferred_element_type=jnp.float32)
    plane_scores[r] = jnp.sum(picked * hot_q, axis=0, keepdims=True)

    def plane_score_copy(s):
        return remote(
            plane_scores.at[r], plane_scores.at[r], ps_send.at[s - 1], ps_recv.at[r], plane_peer(s)
        )

    def column_score_copy(dz):
        return remote(
            column_scores.at[z], column_scores.at[z], cs_send.at[dz - 1], cs_recv.at[z],
            (column_index(dz), b),
        )

    for s in range(1, n_in):
        plane_score_copy(s).start()
    for s in range(1, n_in):
        landed(plane_scores.at[(r + s) % n_in], ps_recv.at[(r + s) % n_in])
    column_scores[z] = jnp.sum(plane_scores[...], axis=0)
    for dz in range(1, n_planes):
        column_score_copy(dz).start()
    for dz in range(1, n_planes):
        landed(column_scores.at[(z + dz) % n_planes], cs_recv.at[(z + dz) % n_planes])
    scores = jnp.sum(column_scores[...], axis=0) * inv_root

    is_live = lax.broadcasted_iota(jnp.int32, (1, slots), 1) < count[0]
    residual = jnp.where(is_live, scores - teacher[...].reshape(1, slots), 0.0)
    error = jnp.sum(residual * residual, axis=1, keepdims=True)
    errors[b] = jnp.broadcast_to(error, errors.shape[1:])
    err_copy = remote(errors.at[b], errors.at[b], err_send.at[0], err_recv.at[0], peer)
    err_copy.start()
    pair_grad = 2.0 * residual * inv_root
    pair_table = lax.dot_general(
        hot_q * pair_grad, hot_p, NT_DIMS, precision=HIGHEST, preferred_element_type=jnp.float32
    )
    high = pair_table.astype(jnp.bfloat16)
    low = (pair_table - high.astype(jnp.float32)).astype(jnp.bfloat16)
    split = jnp.concatenate([high, low], axis=0)

    def terms_copy(t):
        return remote(terms.at[other, t], terms_in.at[t], terms_send.at[t], terms_recv.at[t], peer)

    def terms_step(t):
        both = jnp.dot(split, pas_v[t], preferred_element_type=jnp.float32)
        whole = both[: 2 * queries] + both[2 * queries :]
        terms[0, t] = whole[:queries]
        terms[1, t] = whole[queries:]
        terms_copy(t).start()

    def lgrad_copy(t):
        return remote(
            lgrad.at[t, own_rows], lgrad.at[t, own_rows], lgrad_send.at[t], lgrad_recv.at[t], peer
        )

    def lgrad_step(t):
        landed(terms_in.at[t], terms_recv.at[t])
        query_grad = terms[b, t] + terms_in[t]
        spread = jnp.broadcast_to(query_grad[:, None, :], (queries, QLEN, ct)).reshape(tok, ct)
        lgrad[t, own_rows, :] = (spread * part[t, own_rows, :]).astype(jnp.bfloat16)
        lgrad_copy(t).start()

    @pl.loop(0, 3)
    def _(t):
        terms_step(t)

    @pl.loop(3, tiles)
    def _(t):
        terms_step(t)
        lgrad_step(t - 3)

    @pl.loop(tiles - 3, tiles)
    def _(t):
        lgrad_step(t)

    @pl.loop(0, tiles)
    def _(t):
        landed(lgrad.at[t, peer_rows], lgrad_recv.at[t])

    def hidden_block(j):
        block = pl.ds(pl.multiple_of(j * width, width), width)
        total = jnp.zeros((2 * tok, width), jnp.float32)
        for t in range(tiles):
            total += lax.dot_general(
                lgrad[t], head_v[t, block, :], NT_DIMS, preferred_element_type=jnp.float32
            )
        return total.reshape(2, tok, width)

    def x_copy(zz, s):
        return remote(
            hidden_out.at[zz, s - 1],
            from_plane.at[zz, s - 1],
            x_send.at[zz * (n_in - 1) + s - 1],
            x_recv.at[zz * (n_in - 1) + s - 1],
            plane_peer(s),
        )

    @pl.loop(0, zb * (n_in - 1))
    def _(i):
        s, zz = n_in - 1 - i % (n_in - 1), i // (n_in - 1)
        hidden_out[zz, s - 1] = hidden_block(zz * n_in + (r + s) % n_in).astype(jnp.bfloat16)
        x_copy(zz, s).start()

    def y_copy(zz, half):
        return remote(
            plane_sum.at[zz, half],
            from_column.at[z],
            y_send.at[zz * 2 + half],
            y_recv.at[z],
            ((b * zb + zz) * n_in + r, half),
        )

    def y_here(zz, half):
        return pltpu.make_async_copy(plane_sum.at[zz, half], from_column.at[z], y_recv.at[z])

    def y_is_here(zz, half):
        return jnp.logical_and(b * zb + zz == z, b == half)

    @pl.loop(0, zb)
    def _(zz):
        own_sum[zz] = hidden_block(zz * n_in + r)

    @pl.loop(0, zb)
    def _(zz):
        total = own_sum[zz]
        for s in range(n_in - 1, 0, -1):
            landed(from_plane.at[zz, s - 1], x_recv.at[zz * (n_in - 1) + s - 1])
            total += from_plane[zz, s - 1].astype(jnp.float32)
        plane_sum[zz] = total.astype(jnp.bfloat16)
        for half in range(2):

            @pl.when(y_is_here(zz, half))
            def _():
                y_here(zz, half).start()

            @pl.when(jnp.logical_not(y_is_here(zz, half)))
            def _():
                y_copy(zz, half).start()

    total = jnp.zeros((tok, width), jnp.float32)
    for k in range(n_planes):
        landed(from_column.at[k], y_recv.at[k])
        total += from_column[k].astype(jnp.float32)
    grad_out[...] = total.astype(jnp.bfloat16)

    landed(errors.at[other], err_recv.at[0])
    loss_out[...] = (errors[0] + errors[1]) / (slots * 2)

    for dz in range(1, n_planes):
        column_copy(dz).wait_send()
        column_score_copy(dz).wait_send()

    @pl.when(goal != b)
    def _():
        own_to_peer().wait_send()

    for s in range(1, n_in):
        plane_score_copy(s).wait_send()
        for zz in range(zb):
            x_copy(zz, s).wait_send()
            for half in range(2):
                plane_copy(zz, half, s).wait_send()
    err_copy.wait_send()
    for zz in range(zb):
        for half in range(2):

            @pl.when(jnp.logical_not(y_is_here(zz, half)))
            def _():
                y_copy(zz, half).wait_send()

    @pl.loop(0, tiles)
    def _(t):
        part_copy(t).wait_send()
        pool_copy(t).wait_send()
        terms_copy(t).wait_send()
        lgrad_copy(t).wait_send()


def inner_axis(n_vocab):
    size = 1
    while size * size < n_vocab:
        size *= 2
    return size


def fused(n_vocab, hidden, head_weight, passages, pair_query, pair_passage, pair_count, teacher):
    tok, width = hidden.shape
    rows, cols = head_weight.shape
    pg = passages.shape[0]
    slots = pair_query.shape[0]
    n_in = inner_axis(n_vocab)
    n_planes = n_vocab // n_in
    blocks = rows // width
    zb = blocks // n_in
    ct = math.gcd(cols, 512)
    tiles = cols // ct
    queries = tok // QLEN
    vmem = pl.BlockSpec(memory_space=pltpu.VMEM)
    hbm = pl.BlockSpec(memory_space=pl.ANY)
    bf16, f32 = jnp.bfloat16, jnp.float32
    dma = pltpu.SemaphoreType.DMA
    pooled, grad, loss = pl.pallas_call(
        functools.partial(kernel, n_vocab, n_planes, n_in, tiles),
        out_shape=(
            jax.ShapeDtypeStruct((queries, cols), bf16),
            jax.ShapeDtypeStruct((tok, width), bf16),
            jax.ShapeDtypeStruct((1, 128), f32),
        ),
        in_specs=[vmem, hbm, hbm, vmem, vmem, pl.BlockSpec(memory_space=pltpu.SMEM), vmem],
        out_specs=(vmem, vmem, vmem),
        scratch_shapes=[
            pltpu.VMEM((tiles, rows, ct), bf16),
            pltpu.VMEM((tiles, pg, ct), bf16),
            pltpu.VMEM((zb, 2 * tok, rows // zb), bf16),
            pltpu.VMEM((tiles, 2 * tok, ct), f32),
            pltpu.VMEM((tiles, tok, ct), f32),
            pltpu.VMEM((2, tiles, queries, ct), f32),
            pltpu.VMEM((2, tiles, queries, ct), f32),
            pltpu.VMEM((tiles, queries, ct), f32),
            pltpu.VMEM((tiles, 2 * tok, ct), bf16),
            pltpu.VMEM((zb, n_in - 1, 2, tok, width), bf16),
            pltpu.VMEM((zb, n_in - 1, 2, tok, width), bf16),
            pltpu.VMEM((zb, 2, tok, width), f32),
            pltpu.VMEM((zb, 2, tok, width), bf16),
            pltpu.VMEM((n_planes, tok, width), bf16),
            pltpu.VMEM((n_in, 1, slots), f32),
            pltpu.VMEM((n_planes, 1, slots), f32),
            pltpu.VMEM((2, 1, 128), f32),
            dma((tiles,)), dma((tiles,)),
            dma((n_planes,)), dma((2 * blocks,)), dma((2 * zb * (n_in - 1),)),
            dma((tiles,)), dma((tiles,)), dma((tiles,)), dma((tiles,)),
            dma((tiles,)), dma((tiles,)), dma((tiles,)), dma((tiles,)),
            dma((n_in - 1,)), dma((n_in,)), dma((n_planes - 1,)), dma((n_planes,)),
            dma((1,)), dma((1,)),
            dma((zb * (n_in - 1),)), dma((zb * (n_in - 1),)),
            dma((2 * zb,)), dma((n_planes,)),
        ],
        compiler_params=pltpu.CompilerParams(
            collective_id=0, has_side_effects=True, vmem_limit_bytes=52 * 1024 * 1024
        ),
        cost_estimate=pl.CostEstimate(
            flops=8 * tok * rows * cols,
            bytes_accessed=2 * rows * cols + 2 * pg * cols,
            transcendentals=tok * cols,
        ),
    )(
        hidden, head_weight, passages,
        pair_query, pair_passage, pair_count, teacher,
    )
    return (pooled, grad, loss[0, 0])


def local(n_vocab, n_batch, hidden, head_weight, *rest):
    width, rows, cols = hidden.shape[1], head_weight.shape[0], head_weight.shape[1]
    n_in = inner_axis(n_vocab)
    if (
        n_batch == 2
        and n_vocab % n_in == 0
        and (rows // width) % n_in == 0
        and width % 128 == 0
        and cols % 512 == 0
        and cols >= 2048
        and rows * cols <= 2**23
    ):
        return fused(n_vocab, hidden, head_weight, *rest)
    return plain(hidden, head_weight, *rest)


def solution(mesh):
    in_specs = (
        P("batch", "vocab"),
        P("batch", "vocab"),
        P("batch", "vocab"),
        P("batch"),
        P("batch"),
        P("batch"),
        P("batch"),
    )
    out_specs = (P("batch", "vocab"), P("batch", "vocab"), P())
    body = functools.partial(local, mesh.shape["vocab"], mesh.shape["batch"])
    return jax.shard_map(
        body, mesh=mesh, in_specs=in_specs, out_specs=out_specs, check_vma=False)
```
